32 devices in a mesh: tile: 4 (over z), eval: 8 (over y, x, core).
Axes of the slice: x: 2, y: 2, z: 4, core: 2. Of those that a mesh axis runs over, the one named last changes fastest.
Arguments:
- target_geom: float32 [6, 32, 1024], P(None, 'tile', 'eval'), may hold values from -1 to 1
- eta: float32 [32, 1024], P('tile', 'eval'), may hold values from -3 to 3
- phi: float32 [32, 1024], P('tile', 'eval'), may hold values from -3 to 3
- sources: float32 [4, 4, 4, 256], P('tile', None, None, 'eval')
- group_len: int32 [4, 8], replicated, may hold values from 1 to 32, 160 in all within a row
- owner: int32 [4], replicated, may hold values from 0 to 3, each once
Outputs:
- eta_next: float32 [32, 1024], P('tile', 'eval')
- phi_next: float32 [32, 1024], P('tile', 'eval')
- normal_velocity: float32 [32, 1024], P('tile', 'eval')
The draws below stay inside these ranges and needn't reach their ends.
Inputs may be any that keep to these rules, and one draw needn't show every extreme that they name: owner holds distinct tile rows; round r's group is held by tile row owner[r]. `group_len`: each round has some column with all 32 slots live.
All inputs are finite; a program needn't handle non-finite values.
Results may differ from the reference program's by a relative error of at most 0.0001.
Values sent between devices are 32-bit elements; how exact they have to be, the bound alone decides.
A program may use at most 64 MiB of HBM per device.

```python
import math
import jax
import jax.numpy as jnp
import numpy as np
from jax import lax

SC = 32
ROUNDS = 4
NX = 32
NY = 1024
SRC_COLS = 256
OWNER_ROWS = 4
N_EVAL = 8


def draw_sources(key, part):
    key_pos = jax.random.fold_in(key, 11)
    key_str = jax.random.fold_in(key, 23)
    shape_pos = (OWNER_ROWS, ROUNDS, 3, SRC_COLS)
    shape_str = (OWNER_ROWS, ROUNDS, 1, SRC_COLS)
    factor = (3.0 / (ROUNDS * SRC_COLS)) ** 0.5
    coords = jax.random.uniform(key_pos, shape_pos, jnp.float32, -1.0, 1.0)
    strength = jax.random.uniform(key_str, shape_str, jnp.float32, -1.0, 1.0) * factor
    return jnp.concatenate([coords, strength], axis=2).astype(jnp.float32)


def shard_levels(stream_key, extent, shards, least, top_value):
    def one(axis_at, shards_of):
        steps = jax.random.uniform(jax.random.fold_in(jax.random.fold_in(stream_key, 6), axis_at), (shards_of,), jnp.float32, least / len(shards), top_value / len(shards))
        return jnp.repeat(jnp.exp(steps), extent[axis_at] // shards_of).reshape((-1,) + (1,) * (len(extent) - axis_at - 1))

    level = one(*shards[0])
    for cut in shards[1:]:
        level = level * one(*cut)
    return level


def profile(count, total, most, skew):
    loads = [(1 << 20) // math.isqrt(rank ** skew) + 1 for rank in range(2, count + 1)]
    rest, given = total - most - (count - 1), [1] * (count - 1)
    while rest > 0:
        free = [i for i in range(count - 1) if given[i] < most]
        mass, left = sum([loads[i] for i in free]), rest
        for i in free:
            addition = min(most - given[i], max(1, left * loads[i] // mass), rest)
            given[i] = given[i] + addition
            rest = rest - addition
    return np.array([most] + given)


def uneven(key, number_of, total, limit, skew):
    if number_of == 2:
        one = jax.random.randint(key, (), max(1, total - limit), min(limit, total - 1) + 1)
        return jnp.stack([one, total - one])
    sizes = jnp.asarray(profile(number_of, total, limit, skew), jnp.int32)
    couples = (number_of - 1) // 2
    source_of, taker = sizes[1:1 + 2 * couples:2], sizes[2:2 + 2 * couples:2]
    margin = jnp.minimum(source_of - 1, limit - taker)
    shifted = jax.random.randint(jax.random.fold_in(key, 1), (couples,), 0, 1 << 20) % (margin + 1)
    sizes = sizes.at[1:1 + 2 * couples:2].set(source_of - shifted).at[2:2 + 2 * couples:2].set(taker + shifted)
    return sizes[jax.random.permutation(jax.random.fold_in(key, 2), number_of)]


def centred(key, extent, scale, reach, pieces=(), kind=jnp.bfloat16):
    array = scale * jax.random.normal(key, extent, jnp.float32)
    if pieces:
        array = array * shard_levels(key, extent, pieces, -0.22, 0.18)
    return jnp.clip(array, -reach, reach).astype(kind)


def setup_inputs(seed: int = 0) -> dict:
    seeds = jax.random.split(jax.random.key(seed), 7)
    return {
        "target_geom": jnp.clip(jax.random.uniform(seeds[0], (6, NX, NY), jnp.float32, -1.0, 1.0) * shard_levels(seeds[0], (6, NX, NY), ((1, 4), (2, 8)), -0.4, 0.0), -1.0, 1.0),
        "eta": centred(seeds[1], (NX, NY), 0.5, 3.0, ((0, 4), (1, 8)), jnp.float32),
        "phi": centred(seeds[2], (NX, NY), 0.5, 3.0, ((0, 4), (1, 8)), jnp.float32),
        "sources": draw_sources(jax.random.fold_in(seeds[6], 71), 0),
        "group_len": jax.vmap(lambda own: uneven(own, N_EVAL, N_EVAL * SC * 5 // 8, SC, 2))(jax.random.split(seeds[4], ROUNDS)).reshape((ROUNDS, N_EVAL)).astype(jnp.int32),
        "owner": jax.random.permutation(seeds[5], OWNER_ROWS).astype(jnp.int32),
    }


EPS2 = 0.05

def kernel_sum(targ, src):
    dx = targ[0][None] - src[0][:, None, None]
    dy = targ[1][None] - src[1][:, None, None]
    dz = targ[2][None] - src[2][:, None, None]
    dist2 = dx * dx + dy * dy + dz * dz + EPS2
    numer = targ[3][None] * dx + targ[4][None] * dy + targ[5][None] * dz
    return lax.optimization_barrier(jnp.sum(src[3][:, None, None] * numer / (dist2 * jnp.sqrt(dist2)), axis=0))

def tendency(ext):
    centre = ext[:, 1:-1, 1:-1]
    grad_x = (ext[:, 2:, 1:-1] - ext[:, :-2, 1:-1]) * 0.5
    grad_y = (ext[:, 1:-1, 2:] - ext[:, 1:-1, :-2]) * 0.5
    slope = 1.0 + grad_x[0] * grad_x[0] + grad_y[0] * grad_y[0]
    velocity = centre[2]
    eta_rate = velocity * slope - (grad_x[1] * grad_x[0] + grad_y[1] * grad_y[0])
    phi_rate = -centre[0] - 0.5 * (grad_x[1] * grad_x[1] + grad_y[1] * grad_y[1]) + 0.5 * velocity * velocity * slope
    return jnp.stack([eta_rate, phi_rate])

def smooth(rim):
    centre = rim[:, 1:-1, 1:-1]
    return (4.0 * centre + rim[:, 2:, 1:-1] + rim[:, :-2, 1:-1] + rim[:, 1:-1, 2:] + rim[:, 1:-1, :-2]) / 8.0

def reference(target_geom, eta, phi, sources, group_len, owner):
    slot_ids = jnp.arange(SRC_COLS, dtype=jnp.int32)
    columns = slot_ids // SC
    within = slot_ids % SC
    blocks = []
    for step in range(ROUNDS):
        block = sources[owner[step], step]
        live = (within < group_len[step][columns]).astype(jnp.float32)
        blocks.append(jnp.concatenate([block[:3], block[3:] * live[None]], axis=0))

    def row_velocity(row):
        total = jnp.zeros((1, NY), jnp.float32)
        for block in blocks:
            total = total + kernel_sum(row[:, None, :], block)
        return total[0]
    rows = jnp.moveaxis(target_geom, 1, 0)
    velocity = lax.map(row_velocity, rows)
    fields = jnp.stack([eta, phi, velocity])
    ext = jnp.pad(fields, ((0, 0), (1, 1), (1, 1)))
    rates = tendency(ext)
    rim = jnp.pad(rates, ((0, 0), (1, 1), (1, 1)))
    smoothed = smooth(rim)
    return (eta + 0.5 * smoothed[0], phi + 0.5 * smoothed[1], velocity)
```

```python
import functools

import jax
import jax.numpy as jnp
from jax import lax
from jax.experimental import pallas as pl
from jax.experimental.pallas import tpu as pltpu
from jax.sharding import PartitionSpec as P

ROUNDS = 4
EPS2 = 0.05
HALF = 24
FEATS = 2 * HALF
MESH = pl.DeviceIdType.MESH
F32 = jnp.float32
BF16 = jnp.bfloat16


def split3(v):
    hi = v.astype(BF16).astype(F32)
    rest = v - hi
    mid = rest.astype(BF16).astype(F32)
    low = (rest - mid).astype(BF16).astype(F32)
    return hi, mid, low


def left_six(v):
    a, b, c = split3(v)
    return [a, a, b, a, c, b]


def right_six(v):
    a, b, c = split3(v)
    return [a, b, a, c, a, b]


def target_features(geom):
    x, n = geom[:3], geom[3:]
    one = jnp.ones_like(x[0])
    rows = []
    for c in range(3):
        rows += right_six(x[c])
    rows += list(split3(x[0] * x[0] + x[1] * x[1] + x[2] * x[2] + EPS2))
    rows += [one, one, one]
    for c in range(3):
        rows += right_six(n[c])
    rows += right_six(n[0] * x[0] + n[1] * x[1] + n[2] * x[2])
    return rows


def source_features(y, q):
    one = jnp.ones_like(q)
    rows = []
    for c in range(3):
        rows += left_six(-2.0 * y[c])
    rows += [one, one, one]
    rows += list(split3(y[0] * y[0] + y[1] * y[1] + y[2] * y[2]))
    for c in range(3):
        rows += left_six(-q * y[c])
    rows += left_six(q)
    return rows


def kernel(
    tiles, evals,
    geom, eta, phi, src, glen, owner, out,
    row_out, rows_top, rows_bot, cols_out,
    got, halo_rows, halo_diag, halo_cols,
    tfeat, sfeat, lhs, ext,
    send_src, recv_src, send_halo, recv_halo,
):
    ti, ev = lax.axis_index("tile"), lax.axis_index("eval")
    peers = tiles * evals
    me = ti * evals + ev
    up, down = lax.rem(ti + tiles - 1, tiles), lax.rem(ti + 1, tiles)
    left, right = lax.rem(ev + evals - 1, evals), lax.rem(ev + 1, evals)

    barrier = pltpu.get_barrier_semaphore()

    def greet(k, carry):
        other = lax.rem(me + k, peers)
        pl.semaphore_signal(
            barrier, inc=1,
            device_id=(lax.div(other, evals), lax.rem(other, evals)), device_id_type=MESH,
        )
        return carry

    lax.fori_loop(1, peers, greet, 0)

    width = src.shape[3]
    slot = lax.broadcasted_iota(jnp.int32, (1, width), 1)
    block = jnp.zeros((4, width), F32)
    for r in range(ROUNDS):
        mine = owner[r] == ti
        live = (slot < glen[r, ev]).astype(F32)
        this = src[0, r]
        this = jnp.concatenate([jnp.clip(this[:3], -1e18, 1e18), this[3:] * live], axis=0)
        block = jnp.where(mine, this, block)
    row = jnp.concatenate([block[f:f + 1] for f in range(4)], axis=1)
    row_out[0] = row
    got[me] = row

    height, lanes = eta.shape
    e, p = eta[...], phi[...]
    g = [geom[f] for f in range(6)]
    last = height - 1
    pad = jnp.zeros((6, lanes), F32)
    rows_top[...] = jnp.concatenate(
        [e[0:1], p[0:1], e[1:2], p[1:2]] + [v[0:1] for v in g] + [pad], axis=0)
    rows_bot[...] = jnp.concatenate(
        [e[last:], p[last:], e[last - 1:last], p[last - 1:last]] + [v[last:] for v in g] + [pad],
        axis=0)
    lane = lax.broadcasted_iota(jnp.int32, (height, lanes), 1)
    end = lanes - 1
    columns = [e[:, 0:1], p[:, 0:1], e[:, 1:2], p[:, 1:2]] + [v[:, 0:1] for v in g]
    columns2 = [e[:, end:], p[:, end:], e[:, end - 1:end], p[:, end - 1:end]] + [v[:, end:] for v in g]
    cols = jnp.zeros((height, lanes), F32)
    for k, v in enumerate(columns):
        cols = jnp.where(lane == k, v, cols)
    for k, v in enumerate(columns2):
        cols = jnp.where(lane == 16 + k, v, cols)
    cols_out[...] = cols

    pl.semaphore_wait(barrier, peers - 1)

    def send(k, carry):
        other = lax.rem(me + k, peers)
        pltpu.make_async_remote_copy(
            src_ref=row_out.at[0], dst_ref=got.at[me], send_sem=send_src, recv_sem=recv_src,
            device_id=(lax.div(other, evals), lax.rem(other, evals)), device_id_type=MESH,
        ).start()
        return carry

    lax.fori_loop(1, peers, send, 0)
    first = pl.ds(0, 8)
    plan = [
        (rows_top, halo_rows.at[1], (up, ev)),
        (rows_bot, halo_rows.at[0], (down, ev)),
        (cols_out, halo_cols.at[1], (ti, left)),
        (cols_out, halo_cols.at[0], (ti, right)),
        (rows_top.at[first], halo_diag.at[3], (up, left)),
        (rows_top.at[first], halo_diag.at[2], (up, right)),
        (rows_bot.at[first], halo_diag.at[1], (down, left)),
        (rows_bot.at[first], halo_diag.at[0], (down, right)),
    ]
    copies = []
    for k, (a, b, where) in enumerate(plan):
        copy = pltpu.make_async_remote_copy(
            src_ref=a, dst_ref=b, send_sem=send_halo.at[k], recv_sem=recv_halo.at[k],
            device_id=where, device_id_type=MESH)
        copy.start()
        copies.append(copy)

    for k, v in enumerate(target_features(g)):
        tfeat[0:height, k, :] = v
    ext[...] = jnp.zeros_like(ext)
    for f, v in enumerate((e, p)):
        ext[f, 8:16, 0:lanes] = v

    for copy in copies:
        copy.wait()

    has_up, has_down = ti > 0, ti < tiles - 1
    has_left, has_right = ev > 0, ev < evals - 1
    above, below = halo_rows[0], halo_rows[1]
    near = [jnp.concatenate([above[4 + f:5 + f], below[4 + f:5 + f]], axis=0) for f in range(6)]
    for k, v in enumerate(target_features(near)):
        tfeat[height:height + 2, k, :] = v
    cl, cr = halo_cols[0], halo_cols[1]
    for f in range(2):
        ext[f, 7:8, 0:lanes] = jnp.where(has_up, above[f:f + 1], 0.0)
        ext[f, 6:7, 0:lanes] = jnp.where(has_up, above[2 + f:3 + f], 0.0)
        ext[f, 16:17, 0:lanes] = jnp.where(has_down, below[f:f + 1], 0.0)
        ext[f, 17:18, 0:lanes] = jnp.where(has_down, below[2 + f:3 + f], 0.0)
        lane1 = lane[0:1]

        def side(lf, rt):
            at = lane if lf[0].shape[0] > 1 else lane1
            v = jnp.zeros(at.shape, F32)
            for k, c in enumerate(rt):
                v = jnp.where((at == k) & has_right, c, v)
            for k, c in enumerate(lf):
                v = jnp.where((at == end - k) & has_left, c, v)
            return v

        ext[f, 8:16, lanes:] = side(
            [cl[:, 16 + f:17 + f], cl[:, 18 + f:19 + f]], [cr[:, f:f + 1], cr[:, 2 + f:3 + f]])
        ext[f, 7:8, lanes:] = jnp.where(
            has_up, side([halo_diag[0, f:f + 1, end:]], [halo_diag[1, f:f + 1, 0:1]]), 0.0)
        ext[f, 16:17, lanes:] = jnp.where(
            has_down, side([halo_diag[2, f:f + 1, end:]], [halo_diag[3, f:f + 1, 0:1]]), 0.0)

    others = got.at[pl.ds(0, peers - 1)]
    pltpu.make_async_copy(others, others, recv_src).wait()
    pltpu.make_async_copy(others, others, send_src).wait()

    table = got[:, 0, :]
    if tiles > ROUNDS:
        picked = []
        for r in range(ROUNDS):
            v = jnp.zeros((evals, 4 * width), F32)
            for t in range(tiles):
                v = jnp.where(owner[r] == t, table[t * evals:(t + 1) * evals], v)
            picked.append(v)
        table = jnp.concatenate(picked, axis=0)
    chunks = table.shape[0] // 4
    group = lax.div(lax.broadcasted_iota(jnp.int32, (chunks, 4 * width), 1), width)
    parts = [table[b * chunks:(b + 1) * chunks] for b in range(4)]
    s = []
    for f in range(4):
        v = parts[f]
        for b in range(4):
            if b != f:
                v = jnp.where(group == b, pltpu.roll(parts[b], ((b - f) % 4) * width, 1), v)
        s.append(v)
    y, q = s[:3], s[3]
    for k, v in enumerate(source_features(y, q)):
        sfeat[:, k, :] = v
    wide = 4 * width
    feat = lax.broadcasted_iota(jnp.int32, (wide, FEATS), 1)

    def turn(a, carry):
        t = sfeat[a].T
        lhs[a, 0:wide, :] = jnp.where(feat < HALF, t, 0.0).astype(BF16)
        lhs[a, wide:, :] = jnp.where(feat >= HALF, t, 0.0).astype(BF16)
        return carry

    lax.fori_loop(0, chunks, turn, 0, unroll=min(chunks, 8))

    for n in range(height // 2 + 1):
        rhs = jnp.concatenate([tfeat[2 * n], tfeat[2 * n + 1]], axis=1).astype(BF16)

        def add(a, acc):
            both = jnp.dot(lhs[a], rhs, preferred_element_type=F32)
            dist2, numer = both[:wide], both[wide:]
            r = lax.rsqrt(dist2)
            term = (numer * r) * (r * r)
            return acc + jnp.sum(term.reshape(wide // 8, 8, 2 * lanes), axis=0)

        acc = lax.fori_loop(0, chunks, add, jnp.zeros((8, 2 * lanes), F32), unroll=min(chunks, 8))
        w = jnp.sum(acc, axis=0, keepdims=True)
        if n < height // 2:
            ext[2, 8 + 2 * n:9 + 2 * n, 0:lanes] = w[:, :lanes]
            ext[2, 9 + 2 * n:10 + 2 * n, 0:lanes] = w[:, lanes:]
        else:
            ext[2, 7:8, 0:lanes] = jnp.where(has_up, w[:, :lanes], 0.0)
            ext[2, 16:17, 0:lanes] = jnp.where(has_down, w[:, lanes:], 0.0)

    total = [jnp.zeros((height, wide), F32) for _ in range(2)]
    sides = [[c[:, k:k + 1] for k in range(o, o + 6)] for c, o in ((cl, 20), (cr, 4))]
    sides = [[jnp.broadcast_to(v, (height, wide)) for v in one] for one in sides]
    for a in range(chunks):
        ya = [jnp.broadcast_to(v[a:a + 1], (height, wide)) for v in s]
        for k, t in enumerate(sides):
            d = [t[c] - ya[c] for c in range(3)]
            r = lax.rsqrt(d[0] * d[0] + d[1] * d[1] + d[2] * d[2] + EPS2)
            numer = t[3] * d[0] + t[4] * d[1] + t[5] * d[2]
            total[k] = total[k] + (ya[3] * numer * r) * (r * r)
    wl = jnp.sum(total[0], axis=1, keepdims=True)
    wr = jnp.sum(total[1], axis=1, keepdims=True)
    halo = jnp.where((lane == 0) & has_right, wr, 0.0)
    ext[2, 8:16, lanes:] = jnp.where((lane == end) & has_left, wl, halo)

    span = (24, 2 * lanes)
    ee, pp, ww = ext[0], ext[1], ext[2]
    hi = lambda v, axis: pltpu.roll(v, span[axis] - 1, axis)
    lo = lambda v, axis: pltpu.roll(v, 1, axis)
    grad = lambda v, axis: (hi(v, axis) - lo(v, axis)) * 0.5
    ex, ey, px, py = grad(ee, 0), grad(ee, 1), grad(pp, 0), grad(pp, 1)
    slope = 1.0 + ex * ex + ey * ey
    erate = ww * slope - (px * ex + py * ey)
    prate = -ee - 0.5 * (px * px + py * py) + 0.5 * ww * ww * slope
    ri = lax.broadcasted_iota(jnp.int32, span, 0)
    ci = lax.broadcasted_iota(jnp.int32, span, 1)
    inside = ((ri >= 8) | has_up) & ((ri < 16) | has_down)
    inside = inside & ((ci < lanes) | ((ci < lanes + lanes // 2) & has_right)
                       | ((ci >= lanes + lanes // 2) & has_left))

    def smooth(v):
        v = jnp.where(inside, v, 0.0)
        v = (4.0 * v + hi(v, 0) + lo(v, 0) + hi(v, 1) + lo(v, 1)) * 0.125
        return v[8:16, :lanes]

    out[0] = e + 0.5 * smooth(erate)
    out[1] = p + 0.5 * smooth(prate)
    out[2] = ww[8:16, :lanes]


def body(tiles, evals, target_geom, eta, phi, sources, group_len, owner):
    height, lanes = eta.shape
    width = sources.shape[3]
    chunks = ROUNDS * evals // 4
    vmem = pl.BlockSpec(memory_space=pltpu.VMEM)
    smem = pl.BlockSpec(memory_space=pltpu.SMEM)
    out = pl.pallas_call(
        functools.partial(kernel, tiles, evals),
        out_shape=jax.ShapeDtypeStruct((3, height, lanes), F32),
        in_specs=[vmem] * 4 + [smem] * 2,
        out_specs=vmem,
        scratch_shapes=[
            pltpu.VMEM((1, 1, 4 * width), F32),
            pltpu.VMEM((16, lanes), F32),
            pltpu.VMEM((16, lanes), F32),
            pltpu.VMEM((height, lanes), F32),
            pltpu.VMEM((tiles * evals, 1, 4 * width), F32),
            pltpu.VMEM((2, 16, lanes), F32),
            pltpu.VMEM((4, 8, lanes), F32),
            pltpu.VMEM((2, height, lanes), F32),
            pltpu.VMEM((height + 2, FEATS, lanes), F32),
            pltpu.VMEM((chunks, FEATS, 4 * width), F32),
            pltpu.VMEM((chunks, 8 * width, FEATS), BF16),
            pltpu.VMEM((3, 24, 2 * lanes), F32),
            pltpu.SemaphoreType.DMA,
            pltpu.SemaphoreType.DMA,
            pltpu.SemaphoreType.DMA((8,)),
            pltpu.SemaphoreType.DMA((8,)),
        ],
        compiler_params=pltpu.CompilerParams(
            collective_id=0, has_side_effects=True, vmem_limit_bytes=48 * 1024 * 1024),
    )(target_geom, eta, phi, sources, group_len, owner)
    return out[0], out[1], out[2]


def solution(mesh):
    return jax.shard_map(
        functools.partial(body, mesh.shape["tile"], mesh.shape["eval"]),
        mesh=mesh,
        in_specs=(
            P(None, "tile", "eval"),
            P("tile", "eval"),
            P("tile", "eval"),
            P("tile", None, None, "eval"),
            P(),
            P(),
        ),
        out_specs=(P("tile", "eval"), P("tile", "eval"), P("tile", "eval")),
        check_vma=False,
    )
```

```python
import functools

import jax
import jax.numpy as jnp
from jax import lax
from jax.experimental import pallas as pl
from jax.experimental.pallas import tpu as pltpu
from jax.sharding import PartitionSpec as P

ROUNDS = 4
EPS2 = 0.05
HALF = 24
FEATS = 2 * HALF
MESH = pl.DeviceIdType.MESH
F32 = jnp.float32
BF16 = jnp.bfloat16


def split3(v):
    hi = v.astype(BF16).astype(F32)
    rest = v - hi
    mid = rest.astype(BF16).astype(F32)
    low = (rest - mid).astype(BF16).astype(F32)
    return hi, mid, low


def left_six(v):
    a, b, c = split3(v)
    return [a, a, b, a, c, b]


def right_six(v):
    a, b, c = split3(v)
    return [a, b, a, c, a, b]


def target_features(geom):
    x, n = geom[:3], geom[3:]
    one = jnp.ones_like(x[0])
    rows = []
    for c in range(3):
        rows += right_six(x[c])
    rows += list(split3(x[0] * x[0] + x[1] * x[1] + x[2] * x[2] + EPS2))
    rows += [one, one, one]
    for c in range(3):
        rows += right_six(n[c])
    rows += right_six(n[0] * x[0] + n[1] * x[1] + n[2] * x[2])
    return rows


def source_features(y, q):
    one = jnp.ones_like(q)
    rows = []
    for c in range(3):
        rows += left_six(-2.0 * y[c])
    rows += [one, one, one]
    rows += list(split3(y[0] * y[0] + y[1] * y[1] + y[2] * y[2]))
    for c in range(3):
        rows += left_six(-q * y[c])
    rows += left_six(q)
    return rows


def kernel(
    tiles, evals,
    geom_in, eta_in, phi_in, src_in, glen_in, owner_in, out,
    geom, eta, phi, src, glen, owner, row_out, rows_top, rows_bot, cols_out,
    got, halo_rows, halo_diag, halo_cols,
    tfeat, sfeat, lhs, ext,
    load, send_src, recv_src, send_halo, recv_halo,
):
    pairs = ((src_in, src), (glen_in, glen), (owner_in, owner),
             (geom_in, geom), (eta_in, eta), (phi_in, phi))
    loads = [pltpu.make_async_copy(a, b, load.at[k]) for k, (a, b) in enumerate(pairs)]
    for copy in loads:
        copy.start()
    ti, ev = lax.axis_index("tile"), lax.axis_index("eval")
    peers = tiles * evals
    me = ti * evals + ev
    up, down = lax.rem(ti + tiles - 1, tiles), lax.rem(ti + 1, tiles)
    left, right = lax.rem(ev + evals - 1, evals), lax.rem(ev + 1, evals)

    barrier = pltpu.get_barrier_semaphore()

    def greet(k, carry):
        other = lax.rem(me + k, peers)
        pl.semaphore_signal(
            barrier, inc=1,
            device_id=(lax.div(other, evals), lax.rem(other, evals)), device_id_type=MESH,
        )
        return carry

    lax.fori_loop(1, peers, greet, 0)

    for copy in loads[:3]:
        copy.wait()
    width = src.shape[3]
    slot = lax.broadcasted_iota(jnp.int32, (1, width), 1)
    block = jnp.zeros((4, width), F32)
    for r in range(ROUNDS):
        mine = owner[r] == ti
        live = (slot < glen[r, ev]).astype(F32)
        this = src[0, r]
        this = jnp.concatenate([jnp.clip(this[:3], -1e18, 1e18), this[3:] * live], axis=0)
        block = jnp.where(mine, this, block)
    row = jnp.concatenate([block[f:f + 1] for f in range(4)], axis=1)
    row_out[0] = row
    got[me] = row

    for copy in loads[3:]:
        copy.wait()
    height, lanes = eta.shape
    e, p = eta[...], phi[...]
    g = [geom[f] for f in range(6)]
    last = height - 1
    pad = jnp.zeros((6, lanes), F32)
    rows_top[...] = jnp.concatenate(
        [e[0:1], p[0:1], e[1:2], p[1:2]] + [v[0:1] for v in g] + [pad], axis=0)
    rows_bot[...] = jnp.concatenate(
        [e[last:], p[last:], e[last - 1:last], p[last - 1:last]] + [v[last:] for v in g] + [pad],
        axis=0)
    lane = lax.broadcasted_iota(jnp.int32, (height, lanes), 1)
    end = lanes - 1
    columns = [e[:, 0:1], p[:, 0:1], e[:, 1:2], p[:, 1:2]] + [v[:, 0:1] for v in g]
    columns2 = [e[:, end:], p[:, end:], e[:, end - 1:end], p[:, end - 1:end]] + [v[:, end:] for v in g]
    cols = jnp.zeros((height, lanes), F32)
    for k, v in enumerate(columns):
        cols = jnp.where(lane == k, v, cols)
    for k, v in enumerate(columns2):
        cols = jnp.where(lane == 16 + k, v, cols)
    cols_out[...] = cols

    pl.semaphore_wait(barrier, peers - 1)

    def send(k, carry):
        other = lax.rem(me + k, peers)
        pltpu.make_async_remote_copy(
            src_ref=row_out.at[0], dst_ref=got.at[me], send_sem=send_src, recv_sem=recv_src,
            device_id=(lax.div(other, evals), lax.rem(other, evals)), device_id_type=MESH,
        ).start()
        return carry

    lax.fori_loop(1, peers, send, 0)
    first = pl.ds(0, 8)
    plan = [
        (rows_top, halo_rows.at[1], (up, ev)),
        (rows_bot, halo_rows.at[0], (down, ev)),
        (cols_out, halo_cols.at[1], (ti, left)),
        (cols_out, halo_cols.at[0], (ti, right)),
        (rows_top.at[first], halo_diag.at[3], (up, left)),
        (rows_top.at[first], halo_diag.at[2], (up, right)),
        (rows_bot.at[first], halo_diag.at[1], (down, left)),
        (rows_bot.at[first], halo_diag.at[0], (down, right)),
    ]
    copies = []
    for k, (a, b, where) in enumerate(plan):
        copy = pltpu.make_async_remote_copy(
            src_ref=a, dst_ref=b, send_sem=send_halo.at[k], recv_sem=recv_halo.at[k],
            device_id=where, device_id_type=MESH)
        copy.start()
        copies.append(copy)

    for k, v in enumerate(target_features(g)):
        tfeat[0:height, k, :] = v
    ext[...] = jnp.zeros_like(ext)
    for f, v in enumerate((e, p)):
        ext[f, 8:16, 0:lanes] = v

    others = got.at[pl.ds(0, peers - 1)]
    pltpu.make_async_copy(others, others, recv_src).wait()
    pltpu.make_async_copy(others, others, send_src).wait()

    table = got[:, 0, :]
    if tiles > ROUNDS:
        picked = []
        for r in range(ROUNDS):
            v = jnp.zeros((evals, 4 * width), F32)
            for t in range(tiles):
                v = jnp.where(owner[r] == t, table[t * evals:(t + 1) * evals], v)
            picked.append(v)
        table = jnp.concatenate(picked, axis=0)
    chunks = table.shape[0] // 4
    group = lax.div(lax.broadcasted_iota(jnp.int32, (chunks, 4 * width), 1), width)
    parts = [table[b * chunks:(b + 1) * chunks] for b in range(4)]
    s = []
    for f in range(4):
        v = parts[f]
        for b in range(4):
            if b != f:
                v = jnp.where(group == b, pltpu.roll(parts[b], ((b - f) % 4) * width, 1), v)
        s.append(v)
    y, q = s[:3], s[3]
    for k, v in enumerate(source_features(y, q)):
        sfeat[:, k, :] = v
    wide = 4 * width
    feat = lax.broadcasted_iota(jnp.int32, (wide, FEATS), 1)

    def turn(a, carry):
        t = sfeat[a].T
        lhs[a, 0:wide, :] = jnp.where(feat < HALF, t, 0.0).astype(BF16)
        lhs[a, wide:, :] = jnp.where(feat >= HALF, t, 0.0).astype(BF16)
        return carry

    lax.fori_loop(0, chunks, turn, 0, unroll=min(chunks, 8))

    def velocity(n):
        rhs = jnp.concatenate([tfeat[2 * n], tfeat[2 * n + 1]], axis=1).astype(BF16)

        def add(a, acc):
            both = jnp.dot(lhs[a], rhs, preferred_element_type=F32)
            dist2, numer = both[:wide], both[wide:]
            r = lax.rsqrt(dist2)
            term = (numer * r) * (r * r)
            return acc + jnp.sum(term.reshape(wide // 8, 8, 2 * lanes), axis=0)

        acc = lax.fori_loop(0, chunks, add, jnp.zeros((8, 2 * lanes), F32), unroll=min(chunks, 8))
        return jnp.sum(acc, axis=0, keepdims=True)

    for n in range(height // 2):
        w = velocity(n)
        ext[2, 8 + 2 * n:9 + 2 * n, 0:lanes] = w[:, :lanes]
        ext[2, 9 + 2 * n:10 + 2 * n, 0:lanes] = w[:, lanes:]

    has_up, has_down = ti > 0, ti < tiles - 1
    has_left, has_right = ev > 0, ev < evals - 1
    for copy in copies:
        copy.wait()

    above, below = halo_rows[0], halo_rows[1]
    near = [jnp.concatenate([above[4 + f:5 + f], below[4 + f:5 + f]], axis=0) for f in range(6)]
    for k, v in enumerate(target_features(near)):
        tfeat[height:height + 2, k, :] = v
    cl, cr = halo_cols[0], halo_cols[1]
    for f in range(2):
        ext[f, 7:8, 0:lanes] = jnp.where(has_up, above[f:f + 1], 0.0)
        ext[f, 6:7, 0:lanes] = jnp.where(has_up, above[2 + f:3 + f], 0.0)
        ext[f, 16:17, 0:lanes] = jnp.where(has_down, below[f:f + 1], 0.0)
        ext[f, 17:18, 0:lanes] = jnp.where(has_down, below[2 + f:3 + f], 0.0)
        lane1 = lane[0:1]

        def side(lf, rt):
            at = lane if lf[0].shape[0] > 1 else lane1
            v = jnp.zeros(at.shape, F32)
            for k, c in enumerate(rt):
                v = jnp.where((at == k) & has_right, c, v)
            for k, c in enumerate(lf):
                v = jnp.where((at == end - k) & has_left, c, v)
            return v

        ext[f, 8:16, lanes:] = side(
            [cl[:, 16 + f:17 + f], cl[:, 18 + f:19 + f]], [cr[:, f:f + 1], cr[:, 2 + f:3 + f]])
        ext[f, 7:8, lanes:] = jnp.where(
            has_up, side([halo_diag[0, f:f + 1, end:]], [halo_diag[1, f:f + 1, 0:1]]), 0.0)
        ext[f, 16:17, lanes:] = jnp.where(
            has_down, side([halo_diag[2, f:f + 1, end:]], [halo_diag[3, f:f + 1, 0:1]]), 0.0)

    w = velocity(height // 2)
    ext[2, 7:8, 0:lanes] = jnp.where(has_up, w[:, :lanes], 0.0)
    ext[2, 16:17, 0:lanes] = jnp.where(has_down, w[:, lanes:], 0.0)

    total = [jnp.zeros((height, wide), F32) for _ in range(2)]
    sides = [[c[:, k:k + 1] for k in range(o, o + 6)] for c, o in ((cl, 20), (cr, 4))]
    sides = [[jnp.broadcast_to(v, (height, wide)) for v in one] for one in sides]
    for a in range(chunks):
        ya = [jnp.broadcast_to(v[a:a + 1], (height, wide)) for v in s]
        for k, t in enumerate(sides):
            d = [t[c] - ya[c] for c in range(3)]
            r = lax.rsqrt(d[0] * d[0] + d[1] * d[1] + d[2] * d[2] + EPS2)
            numer = t[3] * d[0] + t[4] * d[1] + t[5] * d[2]
            total[k] = total[k] + (ya[3] * numer * r) * (r * r)
    wl = jnp.sum(total[0], axis=1, keepdims=True)
    wr = jnp.sum(total[1], axis=1, keepdims=True)
    halo = jnp.where((lane == 0) & has_right, wr, 0.0)
    ext[2, 8:16, lanes:] = jnp.where((lane == end) & has_left, wl, halo)

    span = (24, 2 * lanes)
    ee, pp, ww = ext[0], ext[1], ext[2]
    hi = lambda v, axis: pltpu.roll(v, span[axis] - 1, axis)
    lo = lambda v, axis: pltpu.roll(v, 1, axis)
    grad = lambda v, axis: (hi(v, axis) - lo(v, axis)) * 0.5
    ex, ey, px, py = grad(ee, 0), grad(ee, 1), grad(pp, 0), grad(pp, 1)
    slope = 1.0 + ex * ex + ey * ey
    erate = ww * slope - (px * ex + py * ey)
    prate = -ee - 0.5 * (px * px + py * py) + 0.5 * ww * ww * slope
    ri = lax.broadcasted_iota(jnp.int32, span, 0)
    ci = lax.broadcasted_iota(jnp.int32, span, 1)
    inside = ((ri >= 8) | has_up) & ((ri < 16) | has_down)
    inside = inside & ((ci < lanes) | ((ci < lanes + lanes // 2) & has_right)
                       | ((ci >= lanes + lanes // 2) & has_left))

    def smooth(v):
        v = jnp.where(inside, v, 0.0)
        v = (4.0 * v + hi(v, 0) + lo(v, 0) + hi(v, 1) + lo(v, 1)) * 0.125
        return v[8:16, :lanes]

    out[0] = e + 0.5 * smooth(erate)
    out[1] = p + 0.5 * smooth(prate)
    out[2] = ww[8:16, :lanes]


def body(tiles, evals, target_geom, eta, phi, sources, group_len, owner):
    height, lanes = eta.shape
    width = sources.shape[3]
    chunks = ROUNDS * evals // 4
    vmem = pl.BlockSpec(memory_space=pltpu.VMEM)
    hbm = pl.BlockSpec(memory_space=pltpu.HBM)
    out = pl.pallas_call(
        functools.partial(kernel, tiles, evals),
        out_shape=jax.ShapeDtypeStruct((3, height, lanes), F32),
        in_specs=[hbm] * 6,
        out_specs=vmem,
        scratch_shapes=[
            pltpu.VMEM(target_geom.shape, F32),
            pltpu.VMEM(eta.shape, F32),
            pltpu.VMEM(phi.shape, F32),
            pltpu.VMEM(sources.shape, F32),
            pltpu.SMEM(group_len.shape, jnp.int32),
            pltpu.SMEM(owner.shape, jnp.int32),
            pltpu.VMEM((1, 1, 4 * width), F32),
            pltpu.VMEM((16, lanes), F32),
            pltpu.VMEM((16, lanes), F32),
            pltpu.VMEM((height, lanes), F32),
            pltpu.VMEM((tiles * evals, 1, 4 * width), F32),
            pltpu.VMEM((2, 16, lanes), F32),
            pltpu.VMEM((4, 8, lanes), F32),
            pltpu.VMEM((2, height, lanes), F32),
            pltpu.VMEM((height + 2, FEATS, lanes), F32),
            pltpu.VMEM((chunks, FEATS, 4 * width), F32),
            pltpu.VMEM((chunks, 8 * width, FEATS), BF16),
            pltpu.VMEM((3, 24, 2 * lanes), F32),
            pltpu.SemaphoreType.DMA((6,)),
            pltpu.SemaphoreType.DMA,
            pltpu.SemaphoreType.DMA,
            pltpu.SemaphoreType.DMA((8,)),
            pltpu.SemaphoreType.DMA((8,)),
        ],
        compiler_params=pltpu.CompilerParams(
            collective_id=0, has_side_effects=True),
    )(target_geom, eta, phi, sources, group_len, owner)
    return out[0], out[1], out[2]


def solution(mesh):
    return jax.shard_map(
        functools.partial(body, mesh.shape["tile"], mesh.shape["eval"]),
        mesh=mesh,
        in_specs=(
            P(None, "tile", "eval"),
            P("tile", "eval"),
            P("tile", "eval"),
            P("tile", None, None, "eval"),
            P(),
            P(),
        ),
        out_specs=(P("tile", "eval"), P("tile", "eval"), P("tile", "eval")),
        check_vma=False,
    )
```

```python
import functools

import jax
import jax.numpy as jnp
from jax import lax
from jax.experimental import pallas as pl
from jax.experimental.pallas import tpu as pltpu
from jax.sharding import PartitionSpec as P

ROUNDS = 4
EPS2 = 0.05
HALF = 24
FEATS = 2 * HALF
MESH = pl.DeviceIdType.MESH
F32 = jnp.float32
BF16 = jnp.bfloat16


def split3(v):
    hi = v.astype(BF16).astype(F32)
    rest = v - hi
    mid = rest.astype(BF16).astype(F32)
    low = (rest - mid).astype(BF16).astype(F32)
    return hi, mid, low


def left_six(v):
    a, b, c = split3(v)
    return [a, a, b, a, c, b]


def right_six(v):
    a, b, c = split3(v)
    return [a, b, a, c, a, b]


def target_features(geom):
    x, n = geom[:3], geom[3:]
    one = jnp.ones_like(x[0])
    rows = []
    for c in range(3):
        rows += right_six(x[c])
    rows += list(split3(x[0] * x[0] + x[1] * x[1] + x[2] * x[2] + EPS2))
    rows += [one, one, one]
    for c in range(3):
        rows += right_six(n[c])
    rows += right_six(n[0] * x[0] + n[1] * x[1] + n[2] * x[2])
    return rows


def source_features(y, q):
    one = jnp.ones_like(q)
    rows = []
    for c in range(3):
        rows += left_six(-2.0 * y[c])
    rows += [one, one, one]
    rows += list(split3(y[0] * y[0] + y[1] * y[1] + y[2] * y[2]))
    for c in range(3):
        rows += left_six(-q * y[c])
    rows += left_six(q)
    return rows


def kernel(
    tiles, evals,
    geom_in, eta_in, phi_in, src_in, glen_in, owner_in, out,
    geom, eta, phi, src, glen, owner, row_out, rows_top, rows_bot, cols_out,
    got, halo_rows, halo_diag, halo_cols,
    tfeat, sfeat, lhs, ext,
    load, send_src, recv_src, send_halo, recv_halo,
):
    pairs = ((src_in, src), (glen_in, glen), (owner_in, owner),
             (geom_in, geom), (eta_in, eta), (phi_in, phi))
    loads = [pltpu.make_async_copy(a, b, load.at[k]) for k, (a, b) in enumerate(pairs)]
    for copy in loads:
        copy.start()
    ti, ev = lax.axis_index("tile"), lax.axis_index("eval")
    peers = tiles * evals
    me = ti * evals + ev
    up, down = lax.rem(ti + tiles - 1, tiles), lax.rem(ti + 1, tiles)
    left, right = lax.rem(ev + evals - 1, evals), lax.rem(ev + 1, evals)

    barrier = pltpu.get_barrier_semaphore()

    def greet(other, carry):
        pl.semaphore_signal(
            barrier, inc=1,
            device_id=(lax.div(other, evals), lax.rem(other, evals)), device_id_type=MESH,
        )
        return carry

    lax.fori_loop(me + 1, peers, greet, 0)

    for copy in loads[:3]:
        copy.wait()
    width = src.shape[3]
    slot = lax.broadcasted_iota(jnp.int32, (1, width), 1)
    block = jnp.zeros((4, width), F32)
    for r in range(ROUNDS):
        mine = owner[r] == ti
        live = (slot < glen[r, ev]).astype(F32)
        this = src[0, r]
        this = jnp.concatenate([jnp.clip(this[:3], -1e18, 1e18), this[3:] * live], axis=0)
        block = jnp.where(mine, this, block)
    row = jnp.concatenate([block[f:f + 1] for f in range(4)], axis=1)
    row_out[0] = row
    got[me] = row

    for copy in loads[3:]:
        copy.wait()
    height, lanes = eta.shape
    e, p = eta[...], phi[...]
    g = [geom[f] for f in range(6)]
    last = height - 1
    pad = jnp.zeros((6, lanes), F32)
    rows_top[...] = jnp.concatenate(
        [e[0:1], p[0:1], e[1:2], p[1:2]] + [v[0:1] for v in g] + [pad], axis=0)
    rows_bot[...] = jnp.concatenate(
        [e[last:], p[last:], e[last - 1:last], p[last - 1:last]] + [v[last:] for v in g] + [pad],
        axis=0)
    lane = lax.broadcasted_iota(jnp.int32, (height, lanes), 1)
    end = lanes - 1
    columns = [e[:, 0:1], p[:, 0:1], e[:, 1:2], p[:, 1:2]] + [v[:, 0:1] for v in g]
    columns2 = [e[:, end:], p[:, end:], e[:, end - 1:end], p[:, end - 1:end]] + [v[:, end:] for v in g]
    cols = jnp.zeros((height, lanes), F32)
    for k, v in enumerate(columns):
        cols = jnp.where(lane == k, v, cols)
    for k, v in enumerate(columns2):
        cols = jnp.where(lane == 16 + k, v, cols)
    cols_out[...] = cols

    has_up, has_down = ti > 0, ti < tiles - 1
    has_left, has_right = ev > 0, ev < evals - 1

    def send(other):
        pltpu.make_async_remote_copy(
            src_ref=row_out.at[0], dst_ref=got.at[me], send_sem=send_src,
            recv_sem=recv_src.at[me],
            device_id=(lax.div(other, evals), lax.rem(other, evals)), device_id_type=MESH,
        ).start()

    first = pl.ds(0, 8)
    plan = [
        (rows_top, halo_rows.at[1], (up, ev), has_up, has_down),
        (cols_out, halo_cols.at[1], (ti, left), has_left, has_right),
        (rows_top.at[first], halo_diag.at[3], (up, left), has_up & has_left, has_down & has_right),
        (rows_top.at[first], halo_diag.at[2], (up, right), has_up & has_right, has_down & has_left),
        (rows_bot, halo_rows.at[0], (down, ev), has_down, has_up),
        (cols_out, halo_cols.at[0], (ti, right), has_right, has_left),
        (rows_bot.at[first], halo_diag.at[1], (down, left), has_down & has_left, has_up & has_right),
        (rows_bot.at[first], halo_diag.at[0], (down, right), has_down & has_right, has_up & has_left),
    ]
    copies = []
    for k, (a, b, where, sends, takes) in enumerate(plan):
        copy = pltpu.make_async_remote_copy(
            src_ref=a, dst_ref=b, send_sem=send_halo.at[k], recv_sem=recv_halo.at[k],
            device_id=where, device_id_type=MESH)
        copies.append((copy, sends, takes))

    def start(some):
        for copy, sends, _ in some:
            pl.when(sends)(copy.start)

    def send_back(other, carry):
        send(other)
        return carry

    def arrived(d):
        pltpu.make_async_copy(got.at[d], got.at[d], recv_src.at[d]).wait()

    def answer(d, carry):
        arrived(d)
        send(d)
        return carry

    def collect(d, carry):
        arrived(d)
        return carry

    @pl.when(me > 0)
    def _():
        pl.semaphore_wait(barrier, me)

    lax.fori_loop(0, me, send_back, 0)
    start(copies[:4])

    for k, v in enumerate(target_features(g)):
        tfeat[0:height, k, :] = v
    ext[...] = jnp.zeros_like(ext)
    for f, v in enumerate((e, p)):
        ext[f, 8:16, 0:lanes] = v

    near_end = jnp.minimum(me + evals + 2, peers)
    lax.fori_loop(me + 1, near_end, answer, 0)
    start(copies[4:])
    for copy, _, takes in copies:
        pl.when(takes)(copy.wait_recv)

    above, below = halo_rows[0], halo_rows[1]
    near = [jnp.concatenate([above[4 + f:5 + f], below[4 + f:5 + f]], axis=0) for f in range(6)]
    for k, v in enumerate(target_features(near)):
        tfeat[height:height + 2, k, :] = v
    cl, cr = halo_cols[0], halo_cols[1]
    for f in range(2):
        ext[f, 7:8, 0:lanes] = jnp.where(has_up, above[f:f + 1], 0.0)
        ext[f, 6:7, 0:lanes] = jnp.where(has_up, above[2 + f:3 + f], 0.0)
        ext[f, 16:17, 0:lanes] = jnp.where(has_down, below[f:f + 1], 0.0)
        ext[f, 17:18, 0:lanes] = jnp.where(has_down, below[2 + f:3 + f], 0.0)
        lane1 = lane[0:1]

        def side(lf, rt):
            at = lane if lf[0].shape[0] > 1 else lane1
            v = jnp.zeros(at.shape, F32)
            for k, c in enumerate(rt):
                v = jnp.where((at == k) & has_right, c, v)
            for k, c in enumerate(lf):
                v = jnp.where((at == end - k) & has_left, c, v)
            return v

        ext[f, 8:16, lanes:] = side(
            [cl[:, 16 + f:17 + f], cl[:, 18 + f:19 + f]], [cr[:, f:f + 1], cr[:, 2 + f:3 + f]])
        ext[f, 7:8, lanes:] = jnp.where(
            has_up, side([halo_diag[0, f:f + 1, end:]], [halo_diag[1, f:f + 1, 0:1]]), 0.0)
        ext[f, 16:17, lanes:] = jnp.where(
            has_down, side([halo_diag[2, f:f + 1, end:]], [halo_diag[3, f:f + 1, 0:1]]), 0.0)

    wide = 4 * width
    chunks = evals // 4
    group = lax.div(lax.broadcasted_iota(jnp.int32, (chunks, wide), 1), width)
    feat = lax.broadcasted_iota(jnp.int32, (wide, FEATS), 1)
    blocks = height // 2 + 1
    accs = [jnp.zeros((8, 2 * lanes), F32) for _ in range(blocks)]
    total = [jnp.zeros((height, wide), F32) for _ in range(2)]
    sides = [[c[:, k:k + 1] for k in range(o, o + 6)] for c, o in ((cl, 20), (cr, 4))]
    sides = [[jnp.broadcast_to(v, (height, wide)) for v in one] for one in sides]

    def fetch(lo, hi):
        lax.fori_loop(jnp.maximum(near_end, lo), jnp.maximum(near_end, hi), answer, 0)
        lax.fori_loop(jnp.minimum(me, lo), jnp.minimum(me, hi), collect, 0)

    if tiles > ROUNDS:
        fetch(0, peers)
    for step in range(ROUNDS):
        if tiles > ROUNDS:
            table = jnp.zeros((evals, wide), F32)
            for t in range(tiles):
                table = jnp.where(owner[step] == t, got[t * evals:(t + 1) * evals, 0, :], table)
        else:
            fetch(step * evals, (step + 1) * evals)
            table = got[step * evals:(step + 1) * evals, 0, :]
        parts = [table[b * chunks:(b + 1) * chunks] for b in range(4)]
        s = []
        for f in range(4):
            v = parts[f]
            for b in range(4):
                if b != f:
                    v = jnp.where(group == b, pltpu.roll(parts[b], ((b - f) % 4) * width, 1), v)
            s.append(v)
        for k, v in enumerate(source_features(s[:3], s[3])):
            sfeat[step, :, k, :] = v
        for a in range(chunks):
            t = sfeat[step, a].T
            lhs[step, a, 0:wide, :] = jnp.where(feat < HALF, t, 0.0).astype(BF16)
            lhs[step, a, wide:, :] = jnp.where(feat >= HALF, t, 0.0).astype(BF16)

        for n in range(blocks):
            rhs = jnp.concatenate([tfeat[2 * n], tfeat[2 * n + 1]], axis=1).astype(BF16)
            for a in range(chunks):
                both = jnp.dot(lhs[step, a], rhs, preferred_element_type=F32)
                dist2, numer = both[:wide], both[wide:]
                r = lax.rsqrt(dist2)
                term = (numer * r) * (r * r)
                accs[n] = accs[n] + jnp.sum(term.reshape(wide // 8, 8, 2 * lanes), axis=0)

        for a in range(chunks):
            ya = [jnp.broadcast_to(v[a:a + 1], (height, wide)) for v in s]
            for k, t in enumerate(sides):
                d = [t[c] - ya[c] for c in range(3)]
                r = lax.rsqrt(d[0] * d[0] + d[1] * d[1] + d[2] * d[2] + EPS2)
                numer = t[3] * d[0] + t[4] * d[1] + t[5] * d[2]
                total[k] = total[k] + (ya[3] * numer * r) * (r * r)

    for n in range(blocks):
        w = jnp.sum(accs[n], axis=0, keepdims=True)
        if n < height // 2:
            ext[2, 8 + 2 * n:9 + 2 * n, 0:lanes] = w[:, :lanes]
            ext[2, 9 + 2 * n:10 + 2 * n, 0:lanes] = w[:, lanes:]
        else:
            ext[2, 7:8, 0:lanes] = jnp.where(has_up, w[:, :lanes], 0.0)
            ext[2, 16:17, 0:lanes] = jnp.where(has_down, w[:, lanes:], 0.0)
    wl = jnp.sum(total[0], axis=1, keepdims=True)
    wr = jnp.sum(total[1], axis=1, keepdims=True)
    halo = jnp.where((lane == 0) & has_right, wr, 0.0)
    ext[2, 8:16, lanes:] = jnp.where((lane == end) & has_left, wl, halo)

    others = got.at[pl.ds(0, peers - 1)]
    pltpu.make_async_copy(others, others, send_src).wait()
    for copy, sends, _ in copies:
        pl.when(sends)(copy.wait_send)

    span = (24, 2 * lanes)
    ee, pp, ww = ext[0], ext[1], ext[2]
    hi = lambda v, axis: pltpu.roll(v, span[axis] - 1, axis)
    lo = lambda v, axis: pltpu.roll(v, 1, axis)
    grad = lambda v, axis: (hi(v, axis) - lo(v, axis)) * 0.5
    ex, ey, px, py = grad(ee, 0), grad(ee, 1), grad(pp, 0), grad(pp, 1)
    slope = 1.0 + ex * ex + ey * ey
    erate = ww * slope - (px * ex + py * ey)
    prate = -ee - 0.5 * (px * px + py * py) + 0.5 * ww * ww * slope
    ri = lax.broadcasted_iota(jnp.int32, span, 0)
    ci = lax.broadcasted_iota(jnp.int32, span, 1)
    inside = ((ri >= 8) | has_up) & ((ri < 16) | has_down)
    inside = inside & ((ci < lanes) | ((ci < lanes + lanes // 2) & has_right)
                       | ((ci >= lanes + lanes // 2) & has_left))

    def smooth(v):
        v = jnp.where(inside, v, 0.0)
        v = (4.0 * v + hi(v, 0) + lo(v, 0) + hi(v, 1) + lo(v, 1)) * 0.125
        return v[8:16, :lanes]

    out[0] = e + 0.5 * smooth(erate)
    out[1] = p + 0.5 * smooth(prate)
    out[2] = ww[8:16, :lanes]


def body(tiles, evals, target_geom, eta, phi, sources, group_len, owner):
    height, lanes = eta.shape
    width = sources.shape[3]
    chunks = evals // 4
    vmem = pl.BlockSpec(memory_space=pltpu.VMEM)
    hbm = pl.BlockSpec(memory_space=pltpu.HBM)
    out = pl.pallas_call(
        functools.partial(kernel, tiles, evals),
        out_shape=jax.ShapeDtypeStruct((3, height, lanes), F32),
        in_specs=[hbm] * 6,
        out_specs=vmem,
        scratch_shapes=[
            pltpu.VMEM(target_geom.shape, F32),
            pltpu.VMEM(eta.shape, F32),
            pltpu.VMEM(phi.shape, F32),
            pltpu.VMEM(sources.shape, F32),
            pltpu.SMEM(group_len.shape, jnp.int32),
            pltpu.SMEM(owner.shape, jnp.int32),
            pltpu.VMEM((1, 1, 4 * width), F32),
            pltpu.VMEM((16, lanes), F32),
            pltpu.VMEM((16, lanes), F32),
            pltpu.VMEM((height, lanes), F32),
            pltpu.VMEM((tiles * evals, 1, 4 * width), F32),
            pltpu.VMEM((2, 16, lanes), F32),
            pltpu.VMEM((4, 8, lanes), F32),
            pltpu.VMEM((2, height, lanes), F32),
            pltpu.VMEM((height + 2, FEATS, lanes), F32),
            pltpu.VMEM((ROUNDS, chunks, FEATS, 4 * width), F32),
            pltpu.VMEM((ROUNDS, chunks, 8 * width, FEATS), BF16),
            pltpu.VMEM((3, 24, 2 * lanes), F32),
            pltpu.SemaphoreType.DMA((6,)),
            pltpu.SemaphoreType.DMA,
            pltpu.SemaphoreType.DMA((tiles * evals,)),
            pltpu.SemaphoreType.DMA((8,)),
            pltpu.SemaphoreType.DMA((8,)),
        ],
        compiler_params=pltpu.CompilerParams(
            collective_id=0, has_side_effects=True),
    )(target_geom, eta, phi, sources, group_len, owner)
    return out[0], out[1], out[2]


def solution(mesh):
    return jax.shard_map(
        functools.partial(body, mesh.shape["tile"], mesh.shape["eval"]),
        mesh=mesh,
        in_specs=(
            P(None, "tile", "eval"),
            P("tile", "eval"),
            P("tile", "eval"),
            P("tile", None, None, "eval"),
            P(),
            P(),
        ),
        out_specs=(P("tile", "eval"), P("tile", "eval"), P("tile", "eval")),
        check_vma=False,
    )
```

```python
import functools

import jax
import jax.numpy as jnp
from jax import lax
from jax.experimental import pallas as pl
from jax.experimental.pallas import tpu as pltpu
from jax.sharding import PartitionSpec as P

ROUNDS = 4
EPS2 = 0.05
HALF = 24
FEATS = 2 * HALF
MESH = pl.DeviceIdType.MESH
F32 = jnp.float32
BF16 = jnp.bfloat16


def split3(v):
    hi = v.astype(BF16).astype(F32)
    rest = v - hi
    mid = rest.astype(BF16).astype(F32)
    low = (rest - mid).astype(BF16).astype(F32)
    return hi, mid, low


def left_six(v):
    a, b, c = split3(v)
    return [a, a, b, a, c, b]


def right_six(v):
    a, b, c = split3(v)
    return [a, b, a, c, a, b]


def target_features(geom):
    x, n = geom[:3], geom[3:]
    one = jnp.ones_like(x[0])
    rows = []
    for c in range(3):
        rows += right_six(x[c])
    rows += list(split3(x[0] * x[0] + x[1] * x[1] + x[2] * x[2] + EPS2))
    rows += [one, one, one]
    for c in range(3):
        rows += right_six(n[c])
    rows += right_six(n[0] * x[0] + n[1] * x[1] + n[2] * x[2])
    return rows


def source_features(y, q):
    one = jnp.ones_like(q)
    rows = []
    for c in range(3):
        rows += left_six(-2.0 * y[c])
    rows += [one, one, one]
    rows += list(split3(y[0] * y[0] + y[1] * y[1] + y[2] * y[2]))
    for c in range(3):
        rows += left_six(-q * y[c])
    rows += left_six(q)
    return rows


def kernel(
    tiles, evals,
    geom_in, eta_in, phi_in, src_in, glen_in, owner_in, out,
    geom, eta, phi, src, glen, owner, row_out, rows_top, rows_bot, cols_out,
    got, halo_rows, halo_diag, halo_cols,
    tfeat, sfeat, lhs, ext,
    load, send_src, recv_src, send_halo, recv_halo,
):
    pairs = ((src_in, src), (glen_in, glen), (owner_in, owner),
             (geom_in, geom), (eta_in, eta), (phi_in, phi))
    loads = [pltpu.make_async_copy(a, b, load.at[k]) for k, (a, b) in enumerate(pairs)]
    for copy in loads:
        copy.start()
    ti, ev = lax.axis_index("tile"), lax.axis_index("eval")
    peers = tiles * evals
    me = ti * evals + ev
    up, down = lax.rem(ti + tiles - 1, tiles), lax.rem(ti + 1, tiles)
    left, right = lax.rem(ev + evals - 1, evals), lax.rem(ev + 1, evals)

    barrier = pltpu.get_barrier_semaphore()

    def greet(k, carry):
        other = lax.rem(me + k, peers)
        pl.semaphore_signal(
            barrier, inc=1,
            device_id=(lax.div(other, evals), lax.rem(other, evals)), device_id_type=MESH,
        )
        return carry

    lax.fori_loop(1, peers, greet, 0)

    for copy in loads[:3]:
        copy.wait()
    width = src.shape[3]
    slot = lax.broadcasted_iota(jnp.int32, (1, width), 1)
    block = jnp.zeros((4, width), F32)
    for r in range(ROUNDS):
        mine = owner[r] == ti
        live = (slot < glen[r, ev]).astype(F32)
        this = src[0, r]
        this = jnp.concatenate([jnp.clip(this[:3], -1e18, 1e18), this[3:] * live], axis=0)
        block = jnp.where(mine, this, block)
    row = jnp.concatenate([block[f:f + 1] for f in range(4)], axis=1)
    row_out[0] = row
    got[me] = row

    for copy in loads[3:]:
        copy.wait()
    height, lanes = eta.shape
    e, p = eta[...], phi[...]
    g = [geom[f] for f in range(6)]
    last = height - 1
    pad = jnp.zeros((6, lanes), F32)
    rows_top[...] = jnp.concatenate(
        [e[0:1], p[0:1], e[1:2], p[1:2]] + [v[0:1] for v in g] + [pad], axis=0)
    rows_bot[...] = jnp.concatenate(
        [e[last:], p[last:], e[last - 1:last], p[last - 1:last]] + [v[last:] for v in g] + [pad],
        axis=0)
    lane = lax.broadcasted_iota(jnp.int32, (height, lanes), 1)
    end = lanes - 1
    columns = [e[:, 0:1], p[:, 0:1], e[:, 1:2], p[:, 1:2]] + [v[:, 0:1] for v in g]
    columns2 = [e[:, end:], p[:, end:], e[:, end - 1:end], p[:, end - 1:end]] + [v[:, end:] for v in g]
    cols = jnp.zeros((height, lanes), F32)
    for k, v in enumerate(columns):
        cols = jnp.where(lane == k, v, cols)
    for k, v in enumerate(columns2):
        cols = jnp.where(lane == 16 + k, v, cols)
    cols_out[...] = cols

    pl.semaphore_wait(barrier, peers - 1)

    def send(k, carry):
        other = lax.rem(me + k, peers)
        pltpu.make_async_remote_copy(
            src_ref=row_out.at[0], dst_ref=got.at[me], send_sem=send_src, recv_sem=recv_src,
            device_id=(lax.div(other, evals), lax.rem(other, evals)), device_id_type=MESH,
        ).start()
        return carry

    lax.fori_loop(1, peers, send, 0)
    first = pl.ds(0, 8)
    has_up, has_down = ti > 0, ti < tiles - 1
    has_left, has_right = ev > 0, ev < evals - 1
    plan = [
        (rows_top, halo_rows.at[1], (up, ev), has_up, has_down),
        (cols_out, halo_cols.at[1], (ti, left), has_left, has_right),
        (rows_top.at[first], halo_diag.at[3], (up, left), has_up & has_left, has_down & has_right),
        (rows_top.at[first], halo_diag.at[2], (up, right), has_up & has_right, has_down & has_left),
        (rows_bot, halo_rows.at[0], (down, ev), has_down, has_up),
        (cols_out, halo_cols.at[0], (ti, right), has_right, has_left),
        (rows_bot.at[first], halo_diag.at[1], (down, left), has_down & has_left, has_up & has_right),
        (rows_bot.at[first], halo_diag.at[0], (down, right), has_down & has_right, has_up & has_left),
    ]
    copies = []
    for k, (a, b, where, sends, takes) in enumerate(plan):
        copy = pltpu.make_async_remote_copy(
            src_ref=a, dst_ref=b, send_sem=send_halo.at[k], recv_sem=recv_halo.at[k],
            device_id=where, device_id_type=MESH)
        copies.append((copy, sends, takes))

    for copy, sends, _ in copies:
        pl.when(sends)(copy.start)

    for k, v in enumerate(target_features(g)):
        tfeat[0:height, k, :] = v
    ext[...] = jnp.zeros_like(ext)
    for f, v in enumerate((e, p)):
        ext[f, 8:16, 0:lanes] = v

    others = got.at[pl.ds(0, peers - 1)]
    pltpu.make_async_copy(others, others, recv_src).wait()
    pltpu.make_async_copy(others, others, send_src).wait()

    table = got[:, 0, :]
    if tiles > ROUNDS:
        picked = []
        for r in range(ROUNDS):
            v = jnp.zeros((evals, 4 * width), F32)
            for t in range(tiles):
                v = jnp.where(owner[r] == t, table[t * evals:(t + 1) * evals], v)
            picked.append(v)
        table = jnp.concatenate(picked, axis=0)
    chunks = table.shape[0] // 4
    group = lax.div(lax.broadcasted_iota(jnp.int32, (chunks, 4 * width), 1), width)
    parts = [table[b * chunks:(b + 1) * chunks] for b in range(4)]
    s = []
    for f in range(4):
        v = parts[f]
        for b in range(4):
            if b != f:
                v = jnp.where(group == b, pltpu.roll(parts[b], ((b - f) % 4) * width, 1), v)
        s.append(v)
    y, q = s[:3], s[3]
    for k, v in enumerate(source_features(y, q)):
        sfeat[:, k, :] = v
    wide = 4 * width
    feat = lax.broadcasted_iota(jnp.int32, (wide, FEATS), 1)

    def turn(a, carry):
        t = sfeat[a].T
        lhs[a, 0:wide, :] = jnp.where(feat < HALF, t, 0.0).astype(BF16)
        lhs[a, wide:, :] = jnp.where(feat >= HALF, t, 0.0).astype(BF16)
        return carry

    lax.fori_loop(0, chunks, turn, 0, unroll=min(chunks, 8))

    def velocity(n):
        rhs = jnp.concatenate([tfeat[2 * n], tfeat[2 * n + 1]], axis=1).astype(BF16)

        def add(a, acc):
            both = jnp.dot(lhs[a], rhs, preferred_element_type=F32)
            dist2, numer = both[:wide], both[wide:]
            r = lax.rsqrt(dist2)
            term = (numer * r) * (r * r)
            return acc + jnp.sum(term.reshape(wide // 8, 8, 2 * lanes), axis=0)

        acc = lax.fori_loop(0, chunks, add, jnp.zeros((8, 2 * lanes), F32), unroll=min(chunks, 8))
        return jnp.sum(acc, axis=0, keepdims=True)

    for n in range(height // 2):
        w = velocity(n)
        ext[2, 8 + 2 * n:9 + 2 * n, 0:lanes] = w[:, :lanes]
        ext[2, 9 + 2 * n:10 + 2 * n, 0:lanes] = w[:, lanes:]

    for copy, sends, takes in copies:
        pl.when(sends)(copy.wait_send)
        pl.when(takes)(copy.wait_recv)

    above, below = halo_rows[0], halo_rows[1]
    near = [jnp.concatenate([above[4 + f:5 + f], below[4 + f:5 + f]], axis=0) for f in range(6)]
    for k, v in enumerate(target_features(near)):
        tfeat[height:height + 2, k, :] = v
    cl, cr = halo_cols[0], halo_cols[1]
    for f in range(2):
        ext[f, 7:8, 0:lanes] = jnp.where(has_up, above[f:f + 1], 0.0)
        ext[f, 6:7, 0:lanes] = jnp.where(has_up, above[2 + f:3 + f], 0.0)
        ext[f, 16:17, 0:lanes] = jnp.where(has_down, below[f:f + 1], 0.0)
        ext[f, 17:18, 0:lanes] = jnp.where(has_down, below[2 + f:3 + f], 0.0)
        lane1 = lane[0:1]

        def side(lf, rt):
            at = lane if lf[0].shape[0] > 1 else lane1
            v = jnp.zeros(at.shape, F32)
            for k, c in enumerate(rt):
                v = jnp.where((at == k) & has_right, c, v)
            for k, c in enumerate(lf):
                v = jnp.where((at == end - k) & has_left, c, v)
            return v

        ext[f, 8:16, lanes:] = side(
            [cl[:, 16 + f:17 + f], cl[:, 18 + f:19 + f]], [cr[:, f:f + 1], cr[:, 2 + f:3 + f]])
        ext[f, 7:8, lanes:] = jnp.where(
            has_up, side([halo_diag[0, f:f + 1, end:]], [halo_diag[1, f:f + 1, 0:1]]), 0.0)
        ext[f, 16:17, lanes:] = jnp.where(
            has_down, side([halo_diag[2, f:f + 1, end:]], [halo_diag[3, f:f + 1, 0:1]]), 0.0)

    w = velocity(height // 2)
    ext[2, 7:8, 0:lanes] = jnp.where(has_up, w[:, :lanes], 0.0)
    ext[2, 16:17, 0:lanes] = jnp.where(has_down, w[:, lanes:], 0.0)

    total = [jnp.zeros((height, wide), F32) for _ in range(2)]
    sides = [[c[:, k:k + 1] for k in range(o, o + 6)] for c, o in ((cl, 20), (cr, 4))]
    sides = [[jnp.broadcast_to(v, (height, wide)) for v in one] for one in sides]
    for a in range(chunks):
        ya = [jnp.broadcast_to(v[a:a + 1], (height, wide)) for v in s]
        for k, t in enumerate(sides):
            d = [t[c] - ya[c] for c in range(3)]
            r = lax.rsqrt(d[0] * d[0] + d[1] * d[1] + d[2] * d[2] + EPS2)
            numer = t[3] * d[0] + t[4] * d[1] + t[5] * d[2]
            total[k] = total[k] + (ya[3] * numer * r) * (r * r)
    wl = jnp.sum(total[0], axis=1, keepdims=True)
    wr = jnp.sum(total[1], axis=1, keepdims=True)
    halo = jnp.where((lane == 0) & has_right, wr, 0.0)
    ext[2, 8:16, lanes:] = jnp.where((lane == end) & has_left, wl, halo)

    span = (24, 2 * lanes)
    ee, pp, ww = ext[0], ext[1], ext[2]
    hi = lambda v, axis: pltpu.roll(v, span[axis] - 1, axis)
    lo = lambda v, axis: pltpu.roll(v, 1, axis)
    grad = lambda v, axis: (hi(v, axis) - lo(v, axis)) * 0.5
    ex, ey, px, py = grad(ee, 0), grad(ee, 1), grad(pp, 0), grad(pp, 1)
    slope = 1.0 + ex * ex + ey * ey
    erate = ww * slope - (px * ex + py * ey)
    prate = -ee - 0.5 * (px * px + py * py) + 0.5 * ww * ww * slope
    ri = lax.broadcasted_iota(jnp.int32, span, 0)
    ci = lax.broadcasted_iota(jnp.int32, span, 1)
    inside = ((ri >= 8) | has_up) & ((ri < 16) | has_down)
    inside = inside & ((ci < lanes) | ((ci < lanes + lanes // 2) & has_right)
                       | ((ci >= lanes + lanes // 2) & has_left))

    def smooth(v):
        v = jnp.where(inside, v, 0.0)
        v = (4.0 * v + hi(v, 0) + lo(v, 0) + hi(v, 1) + lo(v, 1)) * 0.125
        return v[8:16, :lanes]

    out[0] = e + 0.5 * smooth(erate)
    out[1] = p + 0.5 * smooth(prate)
    out[2] = ww[8:16, :lanes]


def body(tiles, evals, target_geom, eta, phi, sources, group_len, owner):
    height, lanes = eta.shape
    width = sources.shape[3]
    chunks = ROUNDS * evals // 4
    vmem = pl.BlockSpec(memory_space=pltpu.VMEM)
    hbm = pl.BlockSpec(memory_space=pltpu.HBM)
    out = pl.pallas_call(
        functools.partial(kernel, tiles, evals),
        out_shape=jax.ShapeDtypeStruct((3, height, lanes), F32),
        in_specs=[hbm] * 6,
        out_specs=vmem,
        scratch_shapes=[
            pltpu.VMEM(target_geom.shape, F32),
            pltpu.VMEM(eta.shape, F32),
            pltpu.VMEM(phi.shape, F32),
            pltpu.VMEM(sources.shape, F32),
            pltpu.SMEM(group_len.shape, jnp.int32),
            pltpu.SMEM(owner.shape, jnp.int32),
            pltpu.VMEM((1, 1, 4 * width), F32),
            pltpu.VMEM((16, lanes), F32),
            pltpu.VMEM((16, lanes), F32),
            pltpu.VMEM((height, lanes), F32),
            pltpu.VMEM((tiles * evals, 1, 4 * width), F32),
            pltpu.VMEM((2, 16, lanes), F32),
            pltpu.VMEM((4, 8, lanes), F32),
            pltpu.VMEM((2, height, lanes), F32),
            pltpu.VMEM((height + 2, FEATS, lanes), F32),
            pltpu.VMEM((chunks, FEATS, 4 * width), F32),
            pltpu.VMEM((chunks, 8 * width, FEATS), BF16),
            pltpu.VMEM((3, 24, 2 * lanes), F32),
            pltpu.SemaphoreType.DMA((6,)),
            pltpu.SemaphoreType.DMA,
            pltpu.SemaphoreType.DMA,
            pltpu.SemaphoreType.DMA((8,)),
            pltpu.SemaphoreType.DMA((8,)),
        ],
        compiler_params=pltpu.CompilerParams(
            collective_id=0, has_side_effects=True),
    )(target_geom, eta, phi, sources, group_len, owner)
    return out[0], out[1], out[2]


def solution(mesh):
    return jax.shard_map(
        functools.partial(body, mesh.shape["tile"], mesh.shape["eval"]),
        mesh=mesh,
        in_specs=(
            P(None, "tile", "eval"),
            P("tile", "eval"),
            P("tile", "eval"),
            P("tile", None, None, "eval"),
            P(),
            P(),
        ),
        out_specs=(P("tile", "eval"), P("tile", "eval"), P("tile", "eval")),
        check_vma=False,
    )
```
